32 devices in a mesh: section: 2 (over x), shard: 2 (over core), dp: 8 (over z, y).
Axes of the slice: x: 2, y: 2, z: 4, core: 2. Of those that a mesh axis runs over, the one named last changes fastest.
Arguments:
- inputs: bfloat16 [2, 2, 1024, 768], P(None, 'shard', 'dp'), may hold values from -6 to 6
- out_grad: bfloat16 [2, 2, 1024, 768], P(None, 'shard', 'dp'), may hold values from -6 to 6
- doc_lengths: int32 [2, 2, 4], P(None, 'shard'), may hold values from 1 to 897, 1024 in all within a row
- norm_gain: bfloat16 [2, 768], P('section', 'shard'), may hold values from 0.5 to 1.5
- w_z: bfloat16 [2, 768, 1536], P('section', 'shard'), may hold values from -0.21875 to 0.21875
- w_xbc: bfloat16 [2, 768, 1792], P('section', 'shard'), may hold values from -0.21875 to 0.21875
- w_dt: bfloat16 [2, 768, 24], P('section', 'shard'), may hold values from -0.21875 to 0.21875
- conv_w: bfloat16 [2, 4, 1792], P('section', None, 'shard'), may hold values from -3 to 3
- conv_b: bfloat16 [2, 1792], P('section', 'shard'), may hold values from -0.5 to 0.5
- dt_bias: bfloat16 [2, 24], P('section', 'shard'), may hold values from -2 to 0.5
- decay_rate: bfloat16 [2, 24], P('section', 'shard'), may hold values from 0.0009765625 to 0.125
- d_skip: bfloat16 [2, 24], P('section', 'shard'), may hold values from 0.5 to 1.5
- gate_gain: bfloat16 [2, 1536], P('section', 'shard'), may hold values from 0.5 to 1.5
- w_out: bfloat16 [2, 1536, 768], P('section', 'shard'), may hold values from -0.15625 to 0.15625
Outputs:
- activations: bfloat16 [2, 2, 2, 1024, 768], P('section', None, 'shard', 'dp')
- input_grads: bfloat16 [2, 2, 2, 1024, 768], P('section', None, 'shard', 'dp')
- grad_norm_gain: float32 [2, 768], P('section', 'shard')
- grad_w_z: float32 [2, 768, 1536], P('section', 'shard')
- grad_w_xbc: float32 [2, 768, 1792], P('section', 'shard')
- grad_w_dt: float32 [2, 768, 24], P('section', 'shard')
- grad_conv_w: float32 [2, 4, 1792], P('section', None, 'shard')
- grad_conv_b: float32 [2, 1792], P('section', 'shard')
- grad_dt_bias: float32 [2, 24], P('section', 'shard')
- grad_decay_rate: float32 [2, 24], P('section', 'shard')
- grad_d_skip: float32 [2, 24], P('section', 'shard')
- grad_gate_gain: float32 [2, 1536], P('section', 'shard')
- grad_w_out: float32 [2, 1536, 768], P('section', 'shard')
The draws below stay inside these ranges and needn't reach their ends.
Inputs may be any that keep to these rules, and one draw needn't show every extreme that they name: `doc_lengths`: each row of 4 lengths sums to 1024, and its largest length is exactly 897.
All inputs are finite; a program needn't handle non-finite values.
Results may differ from the reference program's by a relative error of at most 0.02.
Values may be sent and summed in bfloat16 or wider, within the bound.
A program may use at most 192 MiB of HBM per device.

```python
import math
from functools import partial
import jax
import jax.numpy as jnp
import numpy as np
from jax import lax

D = 768
DI = 1536
H = 24
P_SIZE = 64
N = 128
KW = 4
XC = 1792
TOK_DEV = 128
MB = 2
NDOC = 4
SEQ = 1024
SEQS = 2
N_SECTION = 2


def steps_of(stream_key, extent, shards, low, largest):
    gain = 1.0
    for position, blocks in shards:
        draws = jax.random.uniform(jax.random.fold_in(jax.random.fold_in(stream_key, 6), position), (blocks,), jnp.float32, low / len(shards), largest / len(shards))
        gain = gain * jnp.repeat(jnp.exp(draws), extent[position] // blocks).reshape((-1,) + (1,) * (len(extent) - 1 - position))
    return gain


def split_up(number_of, total, limit, slope):
    weights = [(1 << 20) // math.isqrt(grade ** slope) + 1 for grade in range(2, number_of + 1)]
    rest, counts = total - limit - (number_of - 1), [1] * (number_of - 1)
    while rest > 0:
        candidates = [i for i in range(number_of - 1) if counts[i] < limit]
        pool, budget = sum([weights[i] for i in candidates]), rest
        for i in candidates:
            addition = min(limit - counts[i], max(1, budget * weights[i] // pool), rest)
            counts[i] = counts[i] + addition
            rest = rest - addition
    return np.array([limit] + counts)


def ragged_sizes(own_key, count, total, bound, lean):
    if count == 2:
        one = jax.random.randint(own_key, (), max(1, total - bound), min(bound, total - 1) + 1)
        return jnp.stack([one, total - one])
    sizes = jnp.asarray(split_up(count, total, bound, lean), jnp.int32)
    couples = (count - 1) // 2
    donor, receiver = sizes[1:1 + 2 * couples:2], sizes[2:2 + 2 * couples:2]
    slack = jnp.minimum(donor - 1, bound - receiver)
    shifted = jax.random.randint(jax.random.fold_in(own_key, 1), (couples,), 0, 1 << 20) % (slack + 1)
    sizes = sizes.at[1:1 + 2 * couples:2].set(donor - shifted).at[2:2 + 2 * couples:2].set(receiver + shifted)
    return sizes[jax.random.permutation(jax.random.fold_in(own_key, 2), count)]


def noise(key, extent, spread, reach, cuts=(), held_as=jnp.bfloat16):
    values = jax.random.normal(key, extent, jnp.float32) * spread
    if len(cuts) > 0:
        values = steps_of(key, extent, cuts, -0.22, 0.18) * values
    return jnp.clip(values, min=-reach, max=reach).astype(held_as)


def setup_inputs(seed: int = 0) -> dict:
    splits = jax.random.split(jax.random.key(seed), 15)
    inputs = noise(splits[0], (MB, SEQS, SEQ, D), 1.0, 6.0, ((1, 2), (2, 8)))
    out_grad = noise(splits[1], (MB, SEQS, SEQ, D), 1.0, 6.0, ((1, 2), (2, 8)))
    doc_lengths = jax.vmap(lambda own: ragged_sizes(own, NDOC, SEQ, SEQ - TOK_DEV + 1, 2))(jax.random.split(splits[2], MB * SEQS)).reshape((MB, SEQS, NDOC)).astype(jnp.int32)
    norm_gain = jnp.clip(1.0 + 0.1 * jax.random.normal(splits[3], (N_SECTION, D), jnp.float32), 0.5, 1.5).astype(jnp.bfloat16)
    w_z = noise(splits[4], (N_SECTION, D, DI), D ** -0.5, 0.21875, ((0, 2), (1, 2)))
    w_xbc = noise(splits[5], (N_SECTION, D, XC), D ** -0.5, 0.21875, ((0, 2), (1, 2)))
    w_dt = noise(splits[6], (N_SECTION, D, H), D ** -0.5, 0.21875, ((0, 2), (1, 2)))
    conv_w = noise(splits[7], (N_SECTION, KW, XC), KW ** -0.5, 3.0, ((0, 2), (2, 2)))
    conv_b = jnp.clip(jax.random.uniform(splits[8], (N_SECTION, XC), jnp.float32, -0.5, 0.5) * steps_of(splits[8], (N_SECTION, XC), ((0, 2), (1, 2)), -0.4, 0.0), -0.5, 0.5).astype(jnp.bfloat16)
    dt_bias = jnp.clip(-2.0 + 2.5 * jax.random.uniform(splits[9], (N_SECTION, H), jnp.float32) ** steps_of(splits[9], (N_SECTION, H), ((0, 2), (1, 2)), -0.2, 0.2), -2.0, 0.5).astype(jnp.bfloat16)
    decay_rate = jnp.clip(jnp.exp(math.log(0.125) - 4.8520303 * jax.random.uniform(splits[10], (N_SECTION, H), jnp.float32) ** steps_of(splits[10], (N_SECTION, H), ((0, 2), (1, 2)), -0.2, 0.2)), 0.0009765625, 0.125).astype(jnp.bfloat16)
    d_skip = jnp.clip(0.5 + 1.0 * jax.random.uniform(splits[11], (N_SECTION, H), jnp.float32) ** steps_of(splits[11], (N_SECTION, H), ((0, 2), (1, 2)), -0.2, 0.2), 0.5, 1.5).astype(jnp.bfloat16)
    gate_gain = jnp.clip(1.0 + 0.1 * jax.random.normal(splits[12], (N_SECTION, DI), jnp.float32), 0.5, 1.5).astype(jnp.bfloat16)
    w_out = noise(splits[13], (N_SECTION, DI, D), DI ** -0.5, 0.15625, ((0, 2), (1, 2)))
    return dict(inputs=inputs, out_grad=out_grad, doc_lengths=doc_lengths, norm_gain=norm_gain, w_z=w_z, w_xbc=w_xbc, w_dt=w_dt, conv_w=conv_w, conv_b=conv_b, dt_bias=dt_bias, decay_rate=decay_rate, d_skip=d_skip, gate_gain=gate_gain, w_out=w_out)


epsilon = 1e-05
highest = lax.Precision.HIGHEST

@jax.custom_vjp
def low(v):
    return lax.optimization_barrier(v.astype(jnp.bfloat16)).astype(jnp.float32)

@jax.custom_vjp
def low_back(v):
    return v

def low_keep(v):
    return (low(v), None)

def low_pass(kept, grad):
    return (grad,)

def back_keep(v):
    return (v, None)

def back_low(kept, grad):
    return (low(grad),)
low.defvjp(low_keep, low_pass)
low_back.defvjp(back_keep, back_low)

def rms_scale(values):
    return values * lax.rsqrt(lax.optimization_barrier(jnp.mean(values * values, axis=-1, keepdims=True)) + epsilon)

def segment_ids(lengths, positions):
    ends = jnp.cumsum(lengths).astype(jnp.int32)
    return lax.optimization_barrier(jnp.sum((positions[:, None] >= ends[None, :]).astype(jnp.int32), axis=1)).astype(jnp.int32)

def ssd_block(state_in, pieces, decay_rate, d_skip):
    xs_block, b_block, c_block, dt_block, seg_block, prior_seg = pieces
    cumul = jnp.cumsum(-dt_block * decay_rate[None, :], axis=0)
    block_size = seg_block.shape[0]
    index_row = jnp.arange(block_size, dtype=jnp.int32)
    keep_mask = ((index_row[:, None] >= index_row[None, :]) & (seg_block[:, None] == seg_block[None, :]))[None]
    cumul_t = cumul.T
    log_gaps = cumul_t[:, :, None] - cumul_t[:, None, :]
    weight = jnp.where(keep_mask, jnp.exp(jnp.where(keep_mask, log_gaps, 0.0)), 0.0)
    inner_cb = jnp.dot(c_block, b_block.T, precision=highest)
    scaled = xs_block * dt_block[:, :, None]
    y_inner = jnp.einsum('hij,jhp->ihp', weight * inner_cb[None], scaled, precision=highest)
    entry_decay = jnp.exp(cumul) * (seg_block == prior_seg)[:, None].astype(jnp.float32)
    y_state = jnp.einsum('in,hpn->ihp', c_block, state_in, precision=highest) * entry_decay[:, :, None]
    output = y_inner + y_state + d_skip[None, :, None] * xs_block
    last_seg = seg_block[-1]
    tail_decay = jnp.exp(cumul[-1][None, :] - cumul) * (seg_block == last_seg)[:, None].astype(jnp.float32)
    through = jnp.exp(cumul[-1]) * (last_seg == prior_seg).astype(jnp.float32)
    fresh_state = jnp.einsum('jhp,jn->hpn', scaled * tail_decay[:, :, None], b_block, precision=highest)
    return (state_in * through[:, None, None] + fresh_state, output)

def mamba_layer(hidden, params, segs):
    norm_gain, w_z, w_xbc, w_dt, conv_w, conv_b, dt_bias, decay_rate, d_skip, gate_gain, w_out = params
    length = hidden.shape[0]
    block_len = min(256, length)
    blocks = length // block_len
    normed_in = low(rms_scale(hidden) * norm_gain[None, :])
    gate_z = low_back(jnp.dot(normed_in, w_z, precision=highest))
    conv_in = low(low_back(jnp.dot(normed_in, w_xbc, precision=highest)))
    dt_raw = low_back(jnp.dot(normed_in, w_dt, precision=highest))
    conv_sum = jnp.broadcast_to(conv_b[None, :], conv_in.shape)
    for tap_no in range(KW):
        lag_rows = KW - 1 - tap_no
        moved = jnp.pad(conv_in, ((lag_rows, 0), (0, 0)))[:length]
        same_doc = jnp.pad(segs, (lag_rows, 0), constant_values=-1)[:length] == segs
        conv_sum = conv_sum + conv_w[tap_no][None, :] * moved * same_doc[:, None].astype(jnp.float32)
    activated = jax.nn.silu(conv_sum)
    xs_all = low(activated[:, :DI]).reshape(blocks, block_len, H, P_SIZE)
    b_all = low(activated[:, DI:DI + N]).reshape(blocks, block_len, N)
    c_all = low(activated[:, DI + N:]).reshape(blocks, block_len, N)
    dt_all = jax.nn.softplus(dt_raw + dt_bias[None, :]).reshape(blocks, block_len, H)
    seg_all = segs.reshape(blocks, block_len)
    priors = jnp.concatenate([jnp.full((1,), -1, jnp.int32), seg_all[:-1, -1].astype(jnp.int32)]).astype(jnp.int32)
    zero_state = jnp.zeros((H, P_SIZE, N), jnp.float32)
    block_fn = jax.checkpoint(partial(ssd_block, decay_rate=decay_rate, d_skip=d_skip))
    unused_state, mixed = lax.scan(block_fn, zero_state, (xs_all, b_all, c_all, dt_all, seg_all, priors))
    y_full = mixed.reshape(length, DI)
    gated = y_full * jax.nn.silu(gate_z)
    normed_out = low(rms_scale(gated) * gate_gain[None, :])
    branch = low_back(jnp.dot(normed_out, w_out, precision=highest))
    return hidden + branch

def reference(inputs, out_grad, doc_lengths, norm_gain, w_z, w_xbc, w_dt, conv_w, conv_b, dt_bias, decay_rate, d_skip, gate_gain, w_out):
    params = tuple((member.astype(jnp.float32) for member in (norm_gain, w_z, w_xbc, w_dt, conv_w, conv_b, dt_bias, decay_rate, d_skip, gate_gain, w_out)))
    first_layer = tuple((member[0] for member in params))
    second_layer = tuple((member[1] for member in params))
    flat_in = inputs.reshape(MB * SEQS, SEQ, D)
    flat_grad = out_grad.reshape(MB * SEQS, SEQ, D)
    flat_len = doc_lengths.reshape(MB * SEQS, NDOC)
    positions = jnp.arange(SEQ, dtype=jnp.int32)

    def one_sequence(carry, item):
        total_zero, total_one = carry
        seq_in, seq_grad, seq_len = item
        segs = segment_ids(seq_len, positions)

        def section_zero(hidden, layer_params):
            return low_back(low(mamba_layer(hidden, layer_params, segs)))

        def section_one(hidden, layer_params):
            return mamba_layer(hidden, layer_params, segs)
        middle, back_zero = jax.vjp(section_zero, seq_in.astype(jnp.float32), first_layer)
        top_out, back_one = jax.vjp(section_one, middle, second_layer)
        grad_middle, grads_one = back_one(seq_grad.astype(jnp.float32))
        grad_in, grads_zero = back_zero(grad_middle)
        total_zero = jax.tree.map(jnp.add, total_zero, grads_zero)
        total_one = jax.tree.map(jnp.add, total_one, grads_one)
        acts = jnp.stack([middle, top_out]).astype(jnp.bfloat16)
        grads_in = jnp.stack([grad_in, grad_middle]).astype(jnp.bfloat16)
        return ((total_zero, total_one), (acts, grads_in))
    zeros_tree = jax.tree.map(jnp.zeros_like, first_layer)
    (total_zero, total_one), (acts, grads_in) = lax.scan(one_sequence, (zeros_tree, zeros_tree), (flat_in, flat_grad, flat_len))
    activations = acts.reshape(MB, SEQS, 2, SEQ, D).transpose(2, 0, 1, 3, 4)
    input_grads = grads_in.reshape(MB, SEQS, 2, SEQ, D).transpose(2, 0, 1, 3, 4)
    stacked = tuple((jnp.stack([first_val, second_val]) for first_val, second_val in zip(total_zero, total_one)))
    return (activations, input_grads, stacked[0], stacked[1], stacked[2], stacked[3], stacked[4], stacked[5], stacked[6], stacked[7], stacked[8], stacked[9], stacked[10])
```

```python
import jax
import jax.numpy as jnp
from jax import lax
from jax.sharding import PartitionSpec as P

DI = 1536
H = 24
P_SIZE = 64
N = 128
KW = 4
XC = 1792


epsilon = 1e-05
high = lax.Precision.HIGH


def passed_along(value, axis, steps):
    count = lax.axis_size(axis)
    first, last = (max(0, -steps), min(count, count - steps))
    return lax.ppermute(value, axis, [(source, source + steps) for source in range(first, last)])


def spans(through_all, upward):
    count, here = (lax.axis_size("dp"), lax.axis_index("dp"))
    spot = jnp.arange(count, dtype=jnp.int32)
    far, mid = (spot[:, None], spot[None, :])
    if upward:
        between, reached = ((mid > here) & (mid < far), spot > here)
    else:
        between, reached = ((mid < here) & (mid > far), spot < here)
    factor = jnp.prod(jnp.where(between[:, :, None], through_all[None], 1.0), axis=1)
    return jnp.where(reached[:, None], factor, 0.0)


def weighted(states, factor):
    return jnp.sum(states.astype(jnp.float32) * factor[:, :, None, None], axis=0)


def entering(through, fresh_state):
    count = lax.axis_size("dp")
    coarse = lax.reduce_precision(through, 8, 7)
    fine = through - coarse
    decays = jnp.pad(jnp.stack([coarse, fine]), ((0, 14), (0, N - H)))
    payload = jnp.concatenate([fresh_state.reshape(H * P_SIZE, N), decays], axis=0)
    everything = lax.all_gather(payload.astype(jnp.bfloat16), "dp")
    states = everything[:, : H * P_SIZE].reshape(count, H, P_SIZE, N)
    halves = everything[:, H * P_SIZE : H * P_SIZE + 2, :H].astype(jnp.float32)
    through_all = halves[:, 0] + halves[:, 1]
    return (weighted(states, spans(through_all, False)), through_all)


def carried_in(grad_state, through_all):
    count = lax.axis_size("dp")
    everything = lax.all_gather(grad_state.reshape(H * P_SIZE, N).astype(jnp.bfloat16), "dp")
    return weighted(everything.reshape(count, H, P_SIZE, N), spans(through_all, True))


def to_owner(whole):
    count = lax.axis_size("shard")
    rows = whole.shape[0] // count
    low = whole.astype(jnp.bfloat16)
    if count != 2:
        return lax.psum_scatter(low, "shard", scatter_dimension=0, tiled=True)
    me = lax.axis_index("shard")
    theirs = lax.dynamic_slice_in_dim(low, (1 - me) * rows, rows, 0)
    own = lax.dynamic_slice_in_dim(low, me * rows, rows, 0)
    got = lax.ppermute(theirs, "shard", [(0, 1), (1, 0)])
    return (own.astype(jnp.float32) + got.astype(jnp.float32)).astype(jnp.bfloat16)


def pack_small(smalls, rows):
    count = lax.axis_size("shard")
    parts = []
    for member in smalls:
        if member.ndim == 2:
            taps, width = member.shape
            member = member.reshape(taps, count, width // count).transpose(1, 0, 2)
        parts.append(member.reshape(count, -1))
    flat = jnp.concatenate(parts, axis=1)
    width = -(-flat.shape[1] // rows)
    flat = jnp.pad(flat, ((0, 0), (0, width * rows - flat.shape[1])))
    return flat.reshape(count * rows, width)


def unpack_small(own, smalls):
    count = lax.axis_size("shard")
    flat = own.reshape(-1)
    start, parts = (0, [])
    for member in smalls:
        shape = member.shape[:-1] + (member.shape[-1] // count,)
        size = member.size // count
        parts.append(flat[start : start + size].reshape(shape))
        start += size
    return parts


def rms_scale(values):
    return values * lax.rsqrt(jnp.mean(values * values, axis=-1, keepdims=True) + epsilon)


def norm_in(hidden, gain):
    return rms_scale(hidden) * gain[None, :]


def segment_ids(lengths, positions):
    ends = jnp.cumsum(lengths)
    return jnp.sum((positions[:, None] >= ends[None, :]).astype(jnp.int32), axis=1)


def col_product(left, right):
    return lax.dot_general(
        left, right, (((0,), (0,)), ((), ())), preferred_element_type=jnp.float32
    )


def row_product(left, right):
    return lax.dot_general(
        left, right, (((1,), (1,)), ((), ())), preferred_element_type=jnp.float32
    )


def conv_gate(extended, dt_raw, conv_w, conv_b, dt_bias, decay_rate, seg_ext):
    tok_rows = dt_raw.shape[0]
    own_seg = seg_ext[KW - 1 :]
    conv_sum = jnp.broadcast_to(conv_b[None, :], (tok_rows, conv_b.shape[0]))
    for tap_no in range(KW):
        same_doc = (seg_ext[tap_no : tap_no + tok_rows] == own_seg)[:, None].astype(jnp.float32)
        conv_sum = (
            conv_sum + conv_w[tap_no][None, :] * extended[tap_no : tap_no + tok_rows] * same_doc
        )
    activated = jax.nn.silu(conv_sum)
    dt_vals = jax.nn.softplus(dt_raw + dt_bias[None, :])
    cumul = jnp.cumsum(-dt_vals * decay_rate[None, :], axis=0)
    return (activated, dt_vals, cumul)


def split_low(activated):
    rounded = activated.astype(jnp.bfloat16).astype(jnp.float32)
    return (rounded[:, :DI], rounded[:, DI : DI + N], rounded[:, DI + N :])


def block_state(xs_vals, b_vals, dt_vals, cumul, own_seg, prior_seg):
    tok_rows = xs_vals.shape[0]
    scaled = xs_vals.reshape(tok_rows, H, P_SIZE) * dt_vals[:, :, None]
    last_seg = own_seg[-1]
    tail_decay = jnp.exp(cumul[-1][None, :] - cumul) * (own_seg == last_seg)[:, None].astype(
        jnp.float32
    )
    fresh_state = jnp.einsum(
        "jhp,jn->hpn", scaled * tail_decay[:, :, None], b_vals, precision=high
    )
    through = jnp.exp(cumul[-1]) * (last_seg == prior_seg).astype(jnp.float32)
    return (through, fresh_state)


def mix_out(
    xs_vals, b_vals, c_vals, dt_vals, cumul, gate_z, state_in, d_skip, gate_gain, own_seg, prior_seg
):
    tok_rows = xs_vals.shape[0]
    heads_x = xs_vals.reshape(tok_rows, H, P_SIZE)
    index_row = jnp.arange(tok_rows, dtype=jnp.int32)
    keep_mask = (
        (index_row[:, None] >= index_row[None, :]) & (own_seg[:, None] == own_seg[None, :])
    )[None]
    cumul_t = cumul.T
    log_gaps = cumul_t[:, :, None] - cumul_t[:, None, :]
    weight = jnp.where(keep_mask, jnp.exp(jnp.where(keep_mask, log_gaps, 0.0)), 0.0)
    inner_cb = jnp.dot(
        c_vals.astype(jnp.bfloat16), b_vals.astype(jnp.bfloat16).T, preferred_element_type=jnp.float32
    )
    scaled = heads_x * dt_vals[:, :, None]
    y_inner = jnp.einsum("hij,jhp->ihp", weight * inner_cb[None], scaled, precision=high)
    entry_decay = jnp.exp(cumul) * (own_seg == prior_seg)[:, None].astype(jnp.float32)
    y_state = (
        jnp.einsum("in,hpn->ihp", c_vals, state_in, precision=high) * entry_decay[:, :, None]
    )
    y_full = (y_inner + y_state + d_skip[None, :, None] * heads_x).reshape(tok_rows, DI)
    gated = y_full * jax.nn.silu(gate_z)
    return rms_scale(gated) * gate_gain[None, :]


def small_params(weights):
    return tuple((weights[index_no].astype(jnp.float32) for index_no in (0, 4, 5, 6, 7, 8, 9)))


def layer_forward(hidden, weights, seg_ext):
    gain_in, conv_wf, conv_bf, bias_f, rate_f, skip_f, ggain_f = small_params(weights)
    tok_rows = hidden.shape[0]
    own_seg = seg_ext[KW - 1 :]
    prior_seg = seg_ext[KW - 2]
    normed_low = norm_in(hidden, gain_in).astype(jnp.bfloat16)
    gate_z = jnp.dot(normed_low, weights[1], preferred_element_type=jnp.float32)
    conv_raw = jnp.dot(normed_low, weights[2], preferred_element_type=jnp.float32).astype(
        jnp.bfloat16
    )
    dt_raw = jnp.dot(normed_low, weights[3], preferred_element_type=jnp.float32)
    rim_rows = passed_along(conv_raw[tok_rows - (KW - 1) :], "dp", 1)
    extended = jnp.concatenate([rim_rows, conv_raw], axis=0).astype(jnp.float32)
    activated, dt_vals, cumul = conv_gate(
        extended, dt_raw, conv_wf, conv_bf, bias_f, rate_f, seg_ext
    )
    xs_vals, b_vals, c_vals = split_low(activated)
    through, fresh_state = block_state(xs_vals, b_vals, dt_vals, cumul, own_seg, prior_seg)
    state_in, through_all = entering(through, fresh_state)
    normed = mix_out(
        xs_vals,
        b_vals,
        c_vals,
        dt_vals,
        cumul,
        gate_z,
        state_in,
        skip_f,
        ggain_f,
        own_seg,
        prior_seg,
    )
    out_low = normed.astype(jnp.bfloat16)
    result = hidden + jnp.dot(out_low, weights[10], preferred_element_type=jnp.float32)
    return (result, (hidden, normed_low, gate_z, extended, dt_raw, state_in, out_low, seg_ext, through_all))


def layer_back(grad_out, kept, weights, valid):
    hidden, normed_low, gate_z, extended, dt_raw, state_in, out_low, seg_ext, through_all = kept
    gain_in, conv_wf, conv_bf, bias_f, rate_f, skip_f, ggain_f = small_params(weights)
    tok_rows = hidden.shape[0]
    own_seg = seg_ext[KW - 1 :]
    prior_seg = seg_ext[KW - 2]
    grad_low = grad_out.astype(jnp.bfloat16)
    grad_normed = row_product(grad_low, weights[10])

    def conv_fn(ext_arg, raw_arg, cw_arg, cb_arg, bias_arg, rate_arg):
        return conv_gate(ext_arg, raw_arg, cw_arg, cb_arg, bias_arg, rate_arg, seg_ext)

    (activated, dt_vals, cumul), conv_back = jax.vjp(
        conv_fn, extended, dt_raw, conv_wf, conv_bf, bias_f, rate_f
    )
    xs_vals, b_vals, c_vals = split_low(activated)

    def mix_fn(xs_arg, b_arg, c_arg, dt_arg, cum_arg, gate_arg, state_arg, skip_arg, ggain_arg):
        return mix_out(
            xs_arg,
            b_arg,
            c_arg,
            dt_arg,
            cum_arg,
            gate_arg,
            state_arg,
            skip_arg,
            ggain_arg,
            own_seg,
            prior_seg,
        )

    normed_unused, mix_back = jax.vjp(
        mix_fn, xs_vals, b_vals, c_vals, dt_vals, cumul, gate_z, state_in, skip_f, ggain_f
    )
    grad_xs, grad_b, grad_c, grad_dt, grad_cum, grad_gate, grad_state, grad_skip, grad_ggain = (
        mix_back(grad_normed)
    )

    def state_fn(xs_arg, b_arg, dt_arg, cum_arg):
        return block_state(xs_arg, b_arg, dt_arg, cum_arg, own_seg, prior_seg)

    (through, fresh_unused), state_back = jax.vjp(state_fn, xs_vals, b_vals, dt_vals, cumul)
    later_grad = carried_in(grad_state, through_all)
    grad_through = jnp.sum(later_grad * state_in, axis=(1, 2))
    more_xs, more_b, more_dt, more_cum = state_back((grad_through, later_grad))
    grad_act = jnp.concatenate([grad_xs + more_xs, grad_b + more_b, grad_c], axis=1)
    grad_ext, grad_raw, grad_cw, grad_cb, grad_bias, grad_rate = conv_back(
        (grad_act, grad_dt + more_dt, grad_cum + more_cum)
    )
    from_next = passed_along(grad_ext[: KW - 1], "dp", -1)
    padding = jnp.zeros((tok_rows - (KW - 1), grad_ext.shape[1]), jnp.float32)
    grad_conv_in = grad_ext[KW - 1 :] + jnp.concatenate([padding, from_next], axis=0)
    gate_low = grad_gate.astype(jnp.bfloat16)
    conv_low = grad_conv_in.astype(jnp.bfloat16)
    step_low = grad_raw.astype(jnp.bfloat16)
    grad_normed_in = (
        row_product(gate_low, weights[1])
        + row_product(conv_low, weights[2])
        + row_product(step_low, weights[3])
    )
    value_unused, norm_back = jax.vjp(norm_in, hidden, gain_in)
    grad_hidden, grad_gain = norm_back(grad_normed_in)
    valid_low = valid.astype(jnp.bfloat16)
    two_low = jnp.concatenate([conv_low, step_low], axis=1)
    pieces = (normed_low * valid_low, gate_low, two_low, out_low * valid_low, grad_low)
    smalls = tuple(
        (
            member * valid
            for member in (grad_gain, grad_cw, grad_cb, grad_bias, grad_rate, grad_skip, grad_ggain)
        )
    )
    return (grad_hidden + grad_out, smalls, pieces)


def per_device(
    inputs,
    out_grad,
    doc_lengths,
    norm_gain,
    w_z,
    w_xbc,
    w_dt,
    conv_w,
    conv_b,
    dt_bias,
    decay_rate,
    d_skip,
    gate_gain,
    w_out,
):
    section_no = lax.axis_index("section")
    is_first = section_no == 0
    micro = inputs.shape[0]
    tok_rows = inputs.shape[2]
    begin = lax.axis_index("dp") * tok_rows
    ext_pos = begin - (KW - 1) + jnp.arange(tok_rows + KW - 1, dtype=jnp.int32)
    gathered = (
        lax.all_gather(norm_gain, "shard", axis=1, tiled=True),
        lax.all_gather(w_z, "shard", axis=1, tiled=True),
        lax.all_gather(w_xbc, "shard", axis=1, tiled=True),
        lax.all_gather(w_dt, "shard", axis=1, tiled=True),
        lax.all_gather(conv_w, "shard", axis=2, tiled=True),
        lax.all_gather(conv_b, "shard", axis=1, tiled=True),
        lax.all_gather(dt_bias, "shard", axis=1, tiled=True),
        lax.all_gather(decay_rate, "shard", axis=1, tiled=True),
        lax.all_gather(d_skip, "shard", axis=1, tiled=True),
        lax.all_gather(gate_gain, "shard", axis=1, tiled=True),
        lax.all_gather(w_out, "shard", axis=1, tiled=True),
    )
    weights = tuple((member[0] for member in gathered))

    def pick(first_val, other_val):
        return jnp.where(is_first, first_val, other_val)

    received = jnp.zeros((tok_rows, inputs.shape[3]), jnp.bfloat16)
    kept_steps = []
    sent_steps = []
    for step_no in range(micro + 1):
        own_rows = inputs[min(step_no, micro - 1), 0]
        hidden = pick(own_rows, received).astype(jnp.float32)
        lengths = pick(doc_lengths[min(step_no, micro - 1), 0], doc_lengths[max(step_no - 1, 0), 0])
        seg_ext = segment_ids(lengths, ext_pos)
        result, kept = layer_forward(hidden, weights, seg_ext)
        sent = result.astype(jnp.bfloat16)
        if step_no < micro:
            received = passed_along(sent, "section", 1)
        kept_steps.append(kept)
        sent_steps.append(sent)
    back_rows = jnp.zeros((tok_rows, inputs.shape[3]), jnp.bfloat16)
    grad_steps = []
    piece_steps = []
    small_total = None
    totals = None
    for step_no in range(micro + 1):
        kept = jax.tree.map(
            pick, kept_steps[max(step_no - 1, 0)], kept_steps[min(step_no + 1, micro)]
        )
        grad_out = pick(back_rows, out_grad[min(step_no, micro - 1), 0]).astype(jnp.float32)
        valid = jnp.where(is_first, step_no >= 1, step_no < micro).astype(jnp.float32)
        grad_hidden, smalls, pieces = layer_back(grad_out, kept, weights, valid)
        grad_low = grad_hidden.astype(jnp.bfloat16)
        if step_no < micro:
            back_rows = passed_along(grad_low, "section", -1)
        grad_steps.append(grad_low)
        piece_steps.append(pieces)
        small_total = (
            smalls
            if small_total is None
            else tuple((left + right for left, right in zip(small_total, smalls)))
        )
    joined = tuple(
        (
            jnp.concatenate([piece[index_no] for piece in piece_steps], axis=0)
            for index_no in range(5)
        )
    )
    left_norm, gate_all, two_all, left_out, grad_all = joined
    own_out = lax.psum(to_owner(col_product(left_out, grad_all)), "dp")
    gate_part = to_owner(col_product(left_norm, gate_all))
    gate_part, own_out = lax.optimization_barrier((gate_part, own_out))
    own_gate = lax.psum(gate_part, "dp")
    small_rows = left_norm.shape[1] // lax.axis_size("shard")
    rest_part = to_owner(
        jnp.concatenate(
            [col_product(left_norm, two_all), pack_small(small_total, small_rows)], axis=1
        )
    )
    rest_part, own_gate = lax.optimization_barrier((rest_part, own_gate))
    own_rest = lax.psum(rest_part, "dp").astype(jnp.float32)
    gains, taps, biases, steps, rates, skips, ggains = unpack_small(
        own_rest[:, XC + H :], small_total
    )
    totals = (
        gains,
        own_gate.astype(jnp.float32),
        own_rest[:, :XC],
        own_rest[:, XC : XC + H],
        taps,
        biases,
        steps,
        rates,
        skips,
        ggains,
        own_out.astype(jnp.float32),
    )
    totals = tuple((member[None] for member in totals))
    activations = jnp.stack(
        [pick(sent_steps[micro_no], sent_steps[micro_no + 1]) for micro_no in range(micro)]
    )
    input_grads = jnp.stack(
        [pick(grad_steps[micro_no + 1], grad_steps[micro_no]) for micro_no in range(micro)]
    )
    activations = activations[None, :, None]
    input_grads = input_grads[None, :, None]
    return (
        activations,
        input_grads,
        totals[0],
        totals[1],
        totals[2],
        totals[3],
        totals[4],
        totals[5],
        totals[6],
        totals[7],
        totals[8],
        totals[9],
        totals[10],
    )


def solution(mesh):
    in_specs = (
        P(None, "shard", "dp", None),
        P(None, "shard", "dp", None),
        P(None, "shard", None),
        P("section", "shard"),
        P("section", "shard", None),
        P("section", "shard", None),
        P("section", "shard", None),
        P("section", None, "shard"),
        P("section", "shard"),
        P("section", "shard"),
        P("section", "shard"),
        P("section", "shard"),
        P("section", "shard"),
        P("section", "shard", None),
    )
    out_specs = (
        P("section", None, "shard", "dp", None),
        P("section", None, "shard", "dp", None),
        P("section", "shard"),
        P("section", "shard", None),
        P("section", "shard", None),
        P("section", "shard", None),
        P("section", None, "shard"),
        P("section", "shard"),
        P("section", "shard"),
        P("section", "shard"),
        P("section", "shard"),
        P("section", "shard"),
        P("section", "shard", None),
    )
    return jax.shard_map(
        per_device, mesh=mesh, in_specs=in_specs, out_specs=out_specs, check_vma=False
    )
```

```python
import jax
import jax.numpy as jnp
from jax import lax
from jax.sharding import PartitionSpec as P

DI = 1536
H = 24
P_SIZE = 64
N = 128
KW = 4
XC = 1792


epsilon = 1e-05
high = lax.Precision.HIGH


def passed_along(value, axis, steps):
    count = lax.axis_size(axis)
    first, last = (max(0, -steps), min(count, count - steps))
    return lax.ppermute(value, axis, [(source, source + steps) for source in range(first, last)])


def spans(through_all, upward):
    count, here = (lax.axis_size("dp"), lax.axis_index("dp"))
    spot = jnp.arange(count, dtype=jnp.int32)
    far, mid = (spot[:, None], spot[None, :])
    if upward:
        between, reached = ((mid > here) & (mid < far), spot > here)
    else:
        between, reached = ((mid < here) & (mid > far), spot < here)
    factor = jnp.prod(jnp.where(between[:, :, None], through_all[None], 1.0), axis=1)
    return jnp.where(reached[:, None], factor, 0.0)


def weighted(states, factor):
    return jnp.sum(states.astype(jnp.float32) * factor[:, :, None, None], axis=0)


def entering(through, fresh_state):
    count = lax.axis_size("dp")
    coarse = lax.reduce_precision(through, 8, 7)
    fine = through - coarse
    decays = jnp.pad(jnp.stack([coarse, fine]), ((0, 14), (0, N - H)))
    payload = jnp.concatenate([fresh_state.reshape(H * P_SIZE, N), decays], axis=0)
    everything = lax.all_gather(payload.astype(jnp.bfloat16), "dp")
    states = everything[:, : H * P_SIZE].reshape(count, H, P_SIZE, N)
    halves = everything[:, H * P_SIZE : H * P_SIZE + 2, :H].astype(jnp.float32)
    through_all = halves[:, 0] + halves[:, 1]
    return (weighted(states, spans(through_all, False)), through_all)


def carried_in(grad_state, through_all):
    count = lax.axis_size("dp")
    everything = lax.all_gather(grad_state.reshape(H * P_SIZE, N).astype(jnp.bfloat16), "dp")
    return weighted(everything.reshape(count, H, P_SIZE, N), spans(through_all, True))


def to_owner(whole):
    count = lax.axis_size("shard")
    rows = whole.shape[0] // count
    low = whole.astype(jnp.bfloat16)
    if count != 2:
        return lax.psum_scatter(low, "shard", scatter_dimension=0, tiled=True)
    me = lax.axis_index("shard")
    theirs = lax.dynamic_slice_in_dim(low, (1 - me) * rows, rows, 0)
    own = lax.dynamic_slice_in_dim(low, me * rows, rows, 0)
    got = lax.ppermute(theirs, "shard", [(0, 1), (1, 0)])
    return (own.astype(jnp.float32) + got.astype(jnp.float32)).astype(jnp.bfloat16)


def pack_small(smalls, rows):
    count = lax.axis_size("shard")
    parts = []
    for member in smalls:
        if member.ndim == 2:
            taps, width = member.shape
            member = member.reshape(taps, count, width // count).transpose(1, 0, 2)
        parts.append(member.reshape(count, -1))
    flat = jnp.concatenate(parts, axis=1)
    width = -(-flat.shape[1] // rows)
    flat = jnp.pad(flat, ((0, 0), (0, width * rows - flat.shape[1])))
    return flat.reshape(count * rows, width)


def unpack_small(own, smalls):
    count = lax.axis_size("shard")
    flat = own.reshape(-1)
    start, parts = (0, [])
    for member in smalls:
        shape = member.shape[:-1] + (member.shape[-1] // count,)
        size = member.size // count
        parts.append(flat[start : start + size].reshape(shape))
        start += size
    return parts


def rms_scale(values):
    return values * lax.rsqrt(jnp.mean(values * values, axis=-1, keepdims=True) + epsilon)


def norm_in(hidden, gain):
    return rms_scale(hidden) * gain[None, :]


def segment_ids(lengths, positions):
    ends = jnp.cumsum(lengths)
    return jnp.sum((positions[:, None] >= ends[None, :]).astype(jnp.int32), axis=1)


def col_product(left, right):
    return lax.dot_general(
        left, right, (((0,), (0,)), ((), ())), preferred_element_type=jnp.float32
    )


def row_product(left, right):
    return lax.dot_general(
        left, right, (((1,), (1,)), ((), ())), preferred_element_type=jnp.float32
    )


def conv_gate(extended, dt_raw, conv_w, conv_b, dt_bias, decay_rate, seg_ext):
    tok_rows = dt_raw.shape[0]
    own_seg = seg_ext[KW - 1 :]
    conv_sum = jnp.broadcast_to(conv_b[None, :], (tok_rows, conv_b.shape[0]))
    for tap_no in range(KW):
        same_doc = (seg_ext[tap_no : tap_no + tok_rows] == own_seg)[:, None].astype(jnp.float32)
        conv_sum = (
            conv_sum + conv_w[tap_no][None, :] * extended[tap_no : tap_no + tok_rows] * same_doc
        )
    activated = jax.nn.silu(conv_sum)
    dt_vals = jax.nn.softplus(dt_raw + dt_bias[None, :])
    cumul = jnp.cumsum(-dt_vals * decay_rate[None, :], axis=0)
    return (activated, dt_vals, cumul)


def split_low(activated):
    rounded = activated.astype(jnp.bfloat16).astype(jnp.float32)
    return (rounded[:, :DI], rounded[:, DI : DI + N], rounded[:, DI + N :])


def block_state(xs_vals, b_vals, dt_vals, cumul, own_seg, prior_seg):
    tok_rows = xs_vals.shape[0]
    scaled = xs_vals.reshape(tok_rows, H, P_SIZE) * dt_vals[:, :, None]
    last_seg = own_seg[-1]
    tail_decay = jnp.exp(cumul[-1][None, :] - cumul) * (own_seg == last_seg)[:, None].astype(
        jnp.float32
    )
    fresh_state = jnp.einsum(
        "jhp,jn->hpn", scaled * tail_decay[:, :, None], b_vals, precision=high
    )
    through = jnp.exp(cumul[-1]) * (last_seg == prior_seg).astype(jnp.float32)
    return (through, fresh_state)


def mix_out(
    xs_vals, b_vals, c_vals, dt_vals, cumul, gate_z, state_in, d_skip, gate_gain, own_seg, prior_seg
):
    tok_rows = xs_vals.shape[0]
    heads_x = xs_vals.reshape(tok_rows, H, P_SIZE)
    index_row = jnp.arange(tok_rows, dtype=jnp.int32)
    keep_mask = (
        (index_row[:, None] >= index_row[None, :]) & (own_seg[:, None] == own_seg[None, :])
    )[None]
    cumul_t = cumul.T
    log_gaps = cumul_t[:, :, None] - cumul_t[:, None, :]
    weight = jnp.where(keep_mask, jnp.exp(jnp.where(keep_mask, log_gaps, 0.0)), 0.0)
    inner_cb = jnp.dot(
        c_vals.astype(jnp.bfloat16), b_vals.astype(jnp.bfloat16).T, preferred_element_type=jnp.float32
    )
    scaled = heads_x * dt_vals[:, :, None]
    y_inner = jnp.einsum("hij,jhp->ihp", weight * inner_cb[None], scaled, precision=high)
    entry_decay = jnp.exp(cumul) * (own_seg == prior_seg)[:, None].astype(jnp.float32)
    y_state = (
        jnp.einsum("in,hpn->ihp", c_vals, state_in, precision=high) * entry_decay[:, :, None]
    )
    y_full = (y_inner + y_state + d_skip[None, :, None] * heads_x).reshape(tok_rows, DI)
    gated = y_full * jax.nn.silu(gate_z)
    return rms_scale(gated) * gate_gain[None, :]


def small_params(weights):
    return tuple((weights[index_no].astype(jnp.float32) for index_no in (0, 4, 5, 6, 7, 8, 9)))


def layer_forward(hidden, weights, seg_ext):
    gain_in, conv_wf, conv_bf, bias_f, rate_f, skip_f, ggain_f = small_params(weights)
    tok_rows = hidden.shape[0]
    own_seg = seg_ext[KW - 1 :]
    prior_seg = seg_ext[KW - 2]
    normed_low = norm_in(hidden, gain_in).astype(jnp.bfloat16)
    gate_z = jnp.dot(normed_low, weights[1], preferred_element_type=jnp.float32)
    conv_raw = jnp.dot(normed_low, weights[2], preferred_element_type=jnp.float32).astype(
        jnp.bfloat16
    )
    dt_raw = jnp.dot(normed_low, weights[3], preferred_element_type=jnp.float32)
    rim_rows = passed_along(conv_raw[tok_rows - (KW - 1) :], "dp", 1)
    extended = jnp.concatenate([rim_rows, conv_raw], axis=0).astype(jnp.float32)
    activated, dt_vals, cumul = conv_gate(
        extended, dt_raw, conv_wf, conv_bf, bias_f, rate_f, seg_ext
    )
    xs_vals, b_vals, c_vals = split_low(activated)
    through, fresh_state = block_state(xs_vals, b_vals, dt_vals, cumul, own_seg, prior_seg)
    state_in, through_all = entering(through, fresh_state)
    normed = mix_out(
        xs_vals,
        b_vals,
        c_vals,
        dt_vals,
        cumul,
        gate_z,
        state_in,
        skip_f,
        ggain_f,
        own_seg,
        prior_seg,
    )
    out_low = normed.astype(jnp.bfloat16)
    result = hidden + jnp.dot(out_low, weights[10], preferred_element_type=jnp.float32)
    return (result, (hidden, normed_low, gate_z, extended, dt_raw, state_in, out_low, seg_ext, through_all))


def layer_back(grad_out, kept, weights, valid):
    hidden, normed_low, gate_z, extended, dt_raw, state_in, out_low, seg_ext, through_all = kept
    gain_in, conv_wf, conv_bf, bias_f, rate_f, skip_f, ggain_f = small_params(weights)
    tok_rows = hidden.shape[0]
    own_seg = seg_ext[KW - 1 :]
    prior_seg = seg_ext[KW - 2]
    grad_low = grad_out.astype(jnp.bfloat16)
    grad_normed = row_product(grad_low, weights[10])

    def conv_fn(ext_arg, raw_arg, cw_arg, cb_arg, bias_arg, rate_arg):
        return conv_gate(ext_arg, raw_arg, cw_arg, cb_arg, bias_arg, rate_arg, seg_ext)

    (activated, dt_vals, cumul), conv_back = jax.vjp(
        conv_fn, extended, dt_raw, conv_wf, conv_bf, bias_f, rate_f
    )
    xs_vals, b_vals, c_vals = split_low(activated)

    def mix_fn(xs_arg, b_arg, c_arg, dt_arg, cum_arg, gate_arg, state_arg, skip_arg, ggain_arg):
        return mix_out(
            xs_arg,
            b_arg,
            c_arg,
            dt_arg,
            cum_arg,
            gate_arg,
            state_arg,
            skip_arg,
            ggain_arg,
            own_seg,
            prior_seg,
        )

    normed_unused, mix_back = jax.vjp(
        mix_fn, xs_vals, b_vals, c_vals, dt_vals, cumul, gate_z, state_in, skip_f, ggain_f
    )
    grad_xs, grad_b, grad_c, grad_dt, grad_cum, grad_gate, grad_state, grad_skip, grad_ggain = (
        mix_back(grad_normed)
    )

    def state_fn(xs_arg, b_arg, dt_arg, cum_arg):
        return block_state(xs_arg, b_arg, dt_arg, cum_arg, own_seg, prior_seg)

    (through, fresh_unused), state_back = jax.vjp(state_fn, xs_vals, b_vals, dt_vals, cumul)
    later_grad = carried_in(grad_state, through_all)
    grad_through = jnp.sum(later_grad * state_in, axis=(1, 2))
    more_xs, more_b, more_dt, more_cum = state_back((grad_through, later_grad))
    grad_act = jnp.concatenate([grad_xs + more_xs, grad_b + more_b, grad_c], axis=1)
    grad_ext, grad_raw, grad_cw, grad_cb, grad_bias, grad_rate = conv_back(
        (grad_act, grad_dt + more_dt, grad_cum + more_cum)
    )
    from_next = passed_along(grad_ext[: KW - 1], "dp", -1)
    padding = jnp.zeros((tok_rows - (KW - 1), grad_ext.shape[1]), jnp.float32)
    grad_conv_in = grad_ext[KW - 1 :] + jnp.concatenate([padding, from_next], axis=0)
    gate_low = grad_gate.astype(jnp.bfloat16)
    conv_low = grad_conv_in.astype(jnp.bfloat16)
    step_low = grad_raw.astype(jnp.bfloat16)
    grad_normed_in = (
        row_product(gate_low, weights[1])
        + row_product(conv_low, weights[2])
        + row_product(step_low, weights[3])
    )
    value_unused, norm_back = jax.vjp(norm_in, hidden, gain_in)
    grad_hidden, grad_gain = norm_back(grad_normed_in)
    valid_low = valid.astype(jnp.bfloat16)
    two_low = jnp.concatenate([conv_low, step_low], axis=1)
    pieces = (normed_low * valid_low, gate_low, two_low, out_low * valid_low, grad_low)
    smalls = tuple(
        (
            member * valid
            for member in (grad_gain, grad_cw, grad_cb, grad_bias, grad_rate, grad_skip, grad_ggain)
        )
    )
    return (grad_hidden + grad_out, smalls, pieces)


def per_device(
    inputs,
    out_grad,
    doc_lengths,
    norm_gain,
    w_z,
    w_xbc,
    w_dt,
    conv_w,
    conv_b,
    dt_bias,
    decay_rate,
    d_skip,
    gate_gain,
    w_out,
):
    section_no = lax.axis_index("section")
    is_first = section_no == 0
    micro = inputs.shape[0]
    tok_rows = inputs.shape[2]
    begin = lax.axis_index("dp") * tok_rows
    ext_pos = begin - (KW - 1) + jnp.arange(tok_rows + KW - 1, dtype=jnp.int32)
    gathered = (
        lax.all_gather(norm_gain, "shard", axis=1, tiled=True),
        lax.all_gather(w_z, "shard", axis=1, tiled=True),
        lax.all_gather(w_xbc, "shard", axis=1, tiled=True),
        lax.all_gather(w_dt, "shard", axis=1, tiled=True),
        lax.all_gather(conv_w, "shard", axis=2, tiled=True),
        lax.all_gather(conv_b, "shard", axis=1, tiled=True),
        lax.all_gather(dt_bias, "shard", axis=1, tiled=True),
        lax.all_gather(decay_rate, "shard", axis=1, tiled=True),
        lax.all_gather(d_skip, "shard", axis=1, tiled=True),
        lax.all_gather(gate_gain, "shard", axis=1, tiled=True),
        lax.all_gather(w_out, "shard", axis=1, tiled=True),
    )
    weights = tuple((member[0] for member in gathered))

    def pick(first_val, other_val):
        return jnp.where(is_first, first_val, other_val)

    received = jnp.zeros((tok_rows, inputs.shape[3]), jnp.bfloat16)
    kept_steps = []
    sent_steps = []
    for step_no in range(micro + 1):
        own_rows = inputs[min(step_no, micro - 1), 0]
        hidden = pick(own_rows, received).astype(jnp.float32)
        lengths = pick(doc_lengths[min(step_no, micro - 1), 0], doc_lengths[max(step_no - 1, 0), 0])
        seg_ext = segment_ids(lengths, ext_pos)
        result, kept = layer_forward(hidden, weights, seg_ext)
        sent = result.astype(jnp.bfloat16)
        if step_no < micro:
            received = passed_along(sent, "section", 1)
        kept_steps.append(kept)
        sent_steps.append(sent)
    back_rows = jnp.zeros((tok_rows, inputs.shape[3]), jnp.bfloat16)
    grad_steps = []
    piece_steps = []
    small_total = None
    totals = None
    for step_no in range(micro + 1):
        kept = jax.tree.map(
            pick, kept_steps[max(step_no - 1, 0)], kept_steps[min(step_no + 1, micro)]
        )
        grad_out = pick(back_rows, out_grad[min(step_no, micro - 1), 0]).astype(jnp.float32)
        valid = jnp.where(is_first, step_no >= 1, step_no < micro).astype(jnp.float32)
        grad_hidden, smalls, pieces = layer_back(grad_out, kept, weights, valid)
        grad_low = grad_hidden.astype(jnp.bfloat16)
        if step_no < micro:
            back_rows = passed_along(grad_low, "section", -1)
        grad_steps.append(grad_low)
        piece_steps.append(pieces)
        small_total = (
            smalls
            if small_total is None
            else tuple((left + right for left, right in zip(small_total, smalls)))
        )
    joined = tuple(
        (
            jnp.concatenate([piece[index_no] for piece in piece_steps], axis=0)
            for index_no in range(5)
        )
    )
    left_norm, gate_all, two_all, left_out, grad_all = joined
    own_out = lax.psum(to_owner(col_product(left_out, grad_all)), "dp")
    gate_part = to_owner(col_product(left_norm, gate_all))
    small_rows = left_norm.shape[1] // lax.axis_size("shard")
    rest_part = to_owner(
        jnp.concatenate(
            [col_product(left_norm, two_all), pack_small(small_total, small_rows)], axis=1
        )
    )
    gate_part, rest_part, own_out = lax.optimization_barrier((gate_part, rest_part, own_out))
    own_gate, own_rest = lax.psum((gate_part, rest_part), "dp")
    own_rest = own_rest.astype(jnp.float32)
    gains, taps, biases, steps, rates, skips, ggains = unpack_small(
        own_rest[:, XC + H :], small_total
    )
    totals = (
        gains,
        own_gate.astype(jnp.float32),
        own_rest[:, :XC],
        own_rest[:, XC : XC + H],
        taps,
        biases,
        steps,
        rates,
        skips,
        ggains,
        own_out.astype(jnp.float32),
    )
    totals = tuple((member[None] for member in totals))
    activations = jnp.stack(
        [pick(sent_steps[micro_no], sent_steps[micro_no + 1]) for micro_no in range(micro)]
    )
    input_grads = jnp.stack(
        [pick(grad_steps[micro_no + 1], grad_steps[micro_no]) for micro_no in range(micro)]
    )
    activations = activations[None, :, None]
    input_grads = input_grads[None, :, None]
    return (
        activations,
        input_grads,
        totals[0],
        totals[1],
        totals[2],
        totals[3],
        totals[4],
        totals[5],
        totals[6],
        totals[7],
        totals[8],
        totals[9],
        totals[10],
    )


def solution(mesh):
    in_specs = (
        P(None, "shard", "dp", None),
        P(None, "shard", "dp", None),
        P(None, "shard", None),
        P("section", "shard"),
        P("section", "shard", None),
        P("section", "shard", None),
        P("section", "shard", None),
        P("section", None, "shard"),
        P("section", "shard"),
        P("section", "shard"),
        P("section", "shard"),
        P("section", "shard"),
        P("section", "shard"),
        P("section", "shard", None),
    )
    out_specs = (
        P("section", None, "shard", "dp", None),
        P("section", None, "shard", "dp", None),
        P("section", "shard"),
        P("section", "shard", None),
        P("section", "shard", None),
        P("section", "shard", None),
        P("section", None, "shard"),
        P("section", "shard"),
        P("section", "shard"),
        P("section", "shard"),
        P("section", "shard"),
        P("section", "shard"),
        P("section", "shard", None),
    )
    return jax.shard_map(
        per_device, mesh=mesh, in_specs=in_specs, out_specs=out_specs, check_vma=False
    )
```
